32 devices in a mesh: dp: 2 (over y), ctx: 16 (over z, x, core).
Axes of the slice: x: 2, y: 2, z: 4, core: 2. Of those that a mesh axis runs over, the one named last changes fastest.
Arguments:
- receptance: bfloat16 [4096, 512], P(('dp', 'ctx')), parts along dimension 0, may hold values from -0.75 to 0.75
- token_key: bfloat16 [4096, 512], P(('dp', 'ctx')), parts along dimension 0, may hold values from -0.75 to 0.75
- token_value: bfloat16 [4096, 512], P(('dp', 'ctx')), parts along dimension 0, may hold values from -0.75 to 0.75
- kappa_raw: bfloat16 [4096, 512], P(('dp', 'ctx')), parts along dimension 0, may hold values from -6 to 6
- removal: bfloat16 [4096, 512], P(('dp', 'ctx')), parts along dimension 0, may hold values from 0.0099487305 to 0.029907227
- decay_rate: float32 [4096, 512], P(('dp', 'ctx')), parts along dimension 0, may hold values from 0 to 1
- shard_length: int32 [32], P(('dp', 'ctx')), parts along dimension 0, may hold values from 32 to 128, as said below
- grad_output: bfloat16 [4096, 512], P(('dp', 'ctx')), parts along dimension 0, may hold values from -0.75 to 0.75
Outputs:
- mixed_out: bfloat16 [4096, 512], P(('dp', 'ctx')), parts along dimension 0
- grad_receptance: bfloat16 [4096, 512], P(('dp', 'ctx')), parts along dimension 0
- grad_key: bfloat16 [4096, 512], P(('dp', 'ctx')), parts along dimension 0
- grad_value: bfloat16 [4096, 512], P(('dp', 'ctx')), parts along dimension 0
The draws below stay inside these ranges and needn't reach their ends.
There are 2 independent parts, one for each index of `dp`. The reference program is written for one: setup_inputs(seed, part) draws one part's arguments, and reference() takes and returns one part's arrays. A program takes and returns all parts, laid end to end along the dimension named above; each array names one. Nothing has to cross between parts.
Inputs may be any that keep to these rules, and one draw needn't show every extreme that they name: `shard_length`: in every draw some shard has all 128 tokens live.
All inputs are finite; a program needn't handle non-finite values.
Results may differ from the reference program's by a relative error of at most 0.0017.
The reference program's roundings to bfloat16 on the way (of `state_low` and `adjoint_low`) count: a program that leaves them out, or rounds other values in their place, can miss the bound.
Values sent between devices are 32-bit elements; how exact they have to be, the bound alone decides.
A program may use at most 192 MiB of HBM per device.

```python
import math
import jax
import jax.numpy as jnp
from jax import lax

H = 8
HS = 64
TOK_DEV = 128
C = 512
SEQ = 2048


def draw_decay_rate(key, part):
    channels = H * HS
    shards = SEQ // TOK_DEV
    keys = jax.random.split(jax.random.fold_in(key, 11), 6)
    slow_share = 0.5
    coarse_estimate = jax.random.uniform(keys[0], (SEQ, channels), jnp.float32, 0.5, 1.5)
    slow = (jax.random.uniform(keys[1], (channels,), jnp.float32) < slow_share).astype(jnp.float32)
    fast_rate = jax.random.uniform(keys[2], (channels,), jnp.float32, 1.0 / 50.0, 1.0 / 30.0)
    baseline_decay = slow * (0.25 / SEQ) + (1.0 - slow) * fast_rate
    multiplier_term = jnp.exp(jax.random.uniform(keys[3], (shards, H), jnp.float32, -math.log(2.0), math.log(2.0)))
    multiplier_term = jnp.repeat(jnp.repeat(multiplier_term, TOK_DEV, axis=0), HS, axis=1)
    marked_positions = jax.random.randint(keys[4], (3,), 0, SEQ)
    removal_strength = jax.random.uniform(keys[5], (3,), jnp.float32, 0.22, 0.69)
    row_entries = jnp.arange(SEQ, dtype=jnp.int32)
    spike_factor = jnp.sum((row_entries[:, None] == marked_positions[None, :]).astype(jnp.float32) * removal_strength[None, :], axis=1)
    return (baseline_decay[None, :] * multiplier_term * coarse_estimate + spike_factor[:, None]).astype(jnp.float32)


def draw_kappa_raw(key, part):
    channels = H * HS
    keys = jax.random.split(jax.random.fold_in(key, 37), 3)
    signs = jnp.where(jax.random.uniform(keys[0], (channels,), jnp.float32) < 0.5, -1.0, 1.0)
    magnitude = jax.random.uniform(keys[1], (channels,), jnp.float32, 1.5, 3.0)
    noise_term = jnp.clip(0.3 * jax.random.normal(keys[2], (SEQ, channels), jnp.float32), -0.9, 0.9)
    direction = (signs * magnitude)[None, :]
    return (direction + noise_term).astype(jnp.bfloat16)


def draw_shard_length(key, part):
    shards = SEQ // TOK_DEV
    length_key = jax.random.fold_in(key, 23)
    lengths = jax.random.randint(length_key, (shards,), TOK_DEV // 4, TOK_DEV + 1)
    full = jax.random.randint(jax.random.fold_in(length_key, 1), (), 0, shards)
    return jnp.where(jnp.arange(shards) == full, TOK_DEV, lengths).astype(jnp.int32)


def block_levels(key, extent, cuts, least, top_value):
    def one(axis_at, parts):
        heights = jax.random.uniform(jax.random.fold_in(jax.random.fold_in(key, 6), axis_at), (parts,), jnp.float32, least / len(cuts), top_value / len(cuts))
        return jnp.repeat(jnp.exp(heights), extent[axis_at] // parts).reshape((-1,) + (1,) * (len(extent) - axis_at - 1))

    level = one(*cuts[0])
    for cut in cuts[1:]:
        level = level * one(*cut)
    return level


def normal_values(key, dims, scale, most, cuts=(), kind=jnp.bfloat16):
    factor_of = block_levels(key, dims, cuts, -0.22, 0.18) if cuts else 1.0
    result = jax.random.normal(key, dims, jnp.float32) * scale * factor_of
    return jnp.minimum(jnp.maximum(result, -most), most).astype(kind)


def setup_inputs(seed: int = 0, part: int = 0) -> dict:
    seeds = jax.random.split(jax.random.key(seed), 9)
    part_splits = jax.random.split(jax.random.fold_in(seeds[8], part), 9)
    return {
        "receptance": normal_values(part_splits[0], (SEQ, C), 0.125, 0.75, ((0, 16),)),
        "token_key": normal_values(part_splits[1], (SEQ, C), 0.125, 0.75, ((0, 16),)),
        "token_value": normal_values(part_splits[2], (SEQ, C), 0.125, 0.75, ((0, 16),)),
        "kappa_raw": draw_kappa_raw(jax.random.fold_in(jax.random.fold_in(seeds[8], part), 71), part),
        "removal": jnp.clip(0.0099487305 + 0.019958496 * jax.random.uniform(part_splits[4], (SEQ, C), jnp.float32) ** block_levels(part_splits[4], (SEQ, C), ((0, 16),), -0.2, 0.2), 0.0099487305, 0.029907227).astype(jnp.bfloat16),
        "decay_rate": draw_decay_rate(jax.random.fold_in(jax.random.fold_in(seeds[8], part), 71), part),
        "shard_length": draw_shard_length(jax.random.fold_in(jax.random.fold_in(seeds[8], part), 71), part),
        "grad_output": normal_values(part_splits[7], (SEQ, C), 0.125, 0.75, ((0, 16),)),
    }


HIGHEST = lax.Precision.HIGHEST

def advance(state, decays, unit_kappa, erase_dir):
    along = jnp.einsum('hvk,hk->hv', state, unit_kappa, precision=HIGHEST)
    return state * decays[:, None, :] - along[:, :, None] * erase_dir[:, None, :]

def retreat(adjoint, decays, unit_kappa, erase_dir):
    along = jnp.einsum('hvk,hk->hv', adjoint, erase_dir, precision=HIGHEST)
    return adjoint * decays[:, None, :] - along[:, :, None] * unit_kappa[:, None, :]

def rank_one(left, right):
    return left[:, :, None] * right[:, None, :]

def lowered(matrix):
    return lax.optimization_barrier(matrix.astype(jnp.bfloat16)).astype(jnp.float32)

def forward_step(state, inputs):
    decays, unit_kappa, erase_dir, read_vec, key_vec, value_vec, grad_vec = inputs
    state = advance(state, decays, unit_kappa, erase_dir) + rank_one(value_vec, key_vec)
    state_low = lowered(state)
    output = jnp.einsum('hvk,hk->hv', state_low, read_vec, precision=HIGHEST)
    grad_read = jnp.einsum('hvk,hv->hk', state_low, grad_vec, precision=HIGHEST)
    return (state, (output, grad_read))

def backward_step(carry, inputs):
    decays, unit_kappa, erase_dir, read_vec, key_vec, value_vec, grad_vec = inputs
    adjoint = carry + rank_one(grad_vec, read_vec)
    adjoint_low = lowered(adjoint)
    grad_val = jnp.einsum('hvk,hk->hv', adjoint_low, key_vec, precision=HIGHEST)
    grad_keys = jnp.einsum('hvk,hv->hk', adjoint_low, value_vec, precision=HIGHEST)
    carry = retreat(adjoint, decays, unit_kappa, erase_dir)
    return (carry, (grad_val, grad_keys))

def reference(receptance, token_key, token_value, kappa_raw, removal, decay_rate, shard_length, grad_output):
    seq = receptance.shape[0]
    position = jnp.arange(seq, dtype=jnp.int32)
    shard = position // TOK_DEV
    limit = jnp.take(shard_length, shard)
    live = (position - shard * TOK_DEV < limit).astype(jnp.float32)[:, None]

    def split(values):
        return values.reshape(seq, H, HS)
    decays = split(jnp.exp(-decay_rate.astype(jnp.float32) * live))
    kappa = split(kappa_raw.astype(jnp.float32))
    unit_kappa = kappa / jnp.sqrt(lax.optimization_barrier(jnp.sum(kappa * kappa, axis=-1, keepdims=True)) + 1e-05)
    erase_dir = split(removal.astype(jnp.float32) * live) * unit_kappa
    read_vec = split(receptance.astype(jnp.float32) * live)
    key_vec = split(token_key.astype(jnp.float32) * live)
    value_vec = split(token_value.astype(jnp.float32) * live)
    grad_vec = split(grad_output.astype(jnp.float32) * live)
    series = (decays, unit_kappa, erase_dir, read_vec, key_vec, value_vec, grad_vec)
    start = jnp.zeros((H, HS, HS), jnp.float32)
    final_state, (mixed, grad_read) = lax.scan(forward_step, start, series)
    final_adjoint, (grad_val, grad_keys) = lax.scan(backward_step, start, series, reverse=True)
    width = H * HS
    return (mixed.reshape(seq, width).astype(jnp.bfloat16), grad_read.reshape(seq, width).astype(jnp.bfloat16), grad_keys.reshape(seq, width).astype(jnp.bfloat16), grad_val.reshape(seq, width).astype(jnp.bfloat16))
```

```python
import functools

import jax
import jax.numpy as jnp
from jax import lax
from jax.experimental import pallas as pl
from jax.experimental.pallas import tpu as pltpu
from jax.sharding import PartitionSpec as P

H = 8
HS = 64
F32 = jnp.float32
BF16 = jnp.bfloat16
NN = (((1,), (0,)), ((), ()))
NT = (((1,), (1,)), ((), ()))


def halves(a):
    high = a.astype(BF16)
    return high, (a - high.astype(F32)).astype(BF16)


def dot3(a, b, dims=NN):
    ah, al = a if isinstance(a, tuple) else halves(a)
    bh, bl = b if isinstance(b, tuple) else halves(b)
    one = functools.partial(lax.dot_general, dimension_numbers=dims, preferred_element_type=F32)
    return one(ah, bh) + (one(ah, bl) + one(al, bh))


def iota(shape, dim):
    return lax.broadcasted_iota(jnp.int32, shape, dim)


def local_kernel(
    len_ref, r_ref, k_ref, v_ref, kap_ref, rem_ref, rate_ref, g_ref,
    rows_ref, maps_ref, xy_ref, w_ref, vg_ref,
):
    T, C = r_ref.shape
    live = (iota((T, 1), 0) < len_ref[0]).astype(F32)
    left = iota((T, 2 * HS), 1) < HS
    units = []
    for p in range(C // (2 * HS)):
        kap = kap_ref[:, p * 128:(p + 1) * 128].astype(F32)
        sq = kap * kap
        sa = jnp.sum(jnp.where(left, sq, 0.0), axis=1, keepdims=True)
        sb = jnp.sum(jnp.where(left, 0.0, sq), axis=1, keepdims=True)
        units.append(kap / jnp.sqrt(jnp.where(left, sa, sb) + 1e-05))
    kap = jnp.concatenate(units, axis=1)
    rate = rate_ref[...] * live
    e = rem_ref[...].astype(F32) * live * kap
    r = r_ref[...].astype(F32) * live
    k = k_ref[...].astype(F32) * live
    v = v_ref[...].astype(F32) * live
    g = g_ref[...].astype(F32) * live
    rows_ref[0] = jnp.exp(-rate)
    rows_ref[1] = kap
    rows_ref[2] = e
    rows_ref[3] = r
    rows_ref[4] = k
    tril = (iota((T, T), 0) >= iota((T, T), 1)).astype(F32)
    cs = lax.dot_general(tril, rate, NN, precision=lax.Precision.HIGHEST, preferred_element_type=F32)
    mid = cs[T // 2 - 1:T // 2, :]
    end = cs[T - 1:T, :]
    grow = jnp.exp(cs - mid)
    kap_c = kap * jnp.exp(mid - cs + rate)
    r_c = r * jnp.exp(mid - cs)
    e_ct = (e * grow).T
    k_ct = (k * grow).T
    kap_0t = (kap * jnp.exp(rate - cs)).T
    r_0t = (r * jnp.exp(-cs)).T
    to_end = jnp.exp(cs - end)
    e_end = e * to_end
    k_end = k * to_end
    e_endt = e_end.T
    vt = v.T
    gt = g.T
    vg_ref[0] = vt
    vg_ref[1] = gt
    whole = jnp.exp(-end)
    strict = iota((T, T), 0) > iota((T, T), 1)
    lower = iota((T, T), 0) >= iota((T, T), 1)
    eye = (iota((T, T), 0) == iota((T, T), 1)).astype(F32)
    eye_h = (iota((HS, HS), 0) == iota((HS, HS), 1)).astype(F32)
    heads = range(C // HS)
    row = lambda a, h: a[:, h * HS:(h + 1) * HS]
    col = lambda a, h: a[h * HS:(h + 1) * HS, :]
    low, mixes, seen = [], [], []
    for h in heads:
        both = dot3(
            jnp.concatenate([row(kap_c, h), row(r_c, h)], axis=0),
            jnp.concatenate([col(e_ct, h), col(k_ct, h)], axis=1),
        )
        low.append(jnp.where(strict, both[:T, :T], 0.0))
        mixes.append(jnp.where(strict, both[:T, T:], 0.0))
        seen.append(jnp.where(lower, both[T:, :T], 0.0))
    inverse = [eye - m for m in low]
    power = low
    size = 2
    while size < T:
        split = [halves(m) for m in power]
        power = [dot3(s, s) for s in split]
        inverse = [i + dot3(i, m) for i, m in zip(inverse, power)]
        size *= 2
    bs = []
    for h in heads:
        inv = halves(inverse[h])
        q = halves(seen[h])
        nvt = dot3(col(vt, h), mixes[h], NT)
        xy = dot3(jnp.concatenate([col(kap_0t, h), nvt], axis=0), inv, NT)
        xy_ref[h] = xy
        pa = dot3(xy, row(e_end, h))
        a = dot3(col(vt, h), row(k_end, h)) - pa[HS:]
        prod = eye_h * row(whole, h) - pa[:HS]
        maps_ref[h] = jnp.concatenate([prod, a], axis=1)
        zt = col(r_0t, h) - dot3(xy[:HS], q, NT)
        bs.append(dot3(col(gt, h), zt, NT))
        gq = dot3(col(gt, h), q)
        w_ref[h] = dot3(jnp.concatenate([col(e_endt, h), gq], axis=0), inv)
    for p in range(len(bs) // 2):
        maps_ref[len(bs) + p] = jnp.concatenate([bs[2 * p], bs[2 * p + 1]], axis=1)


def exact_kernel(
    place_ref, gath_ref, rows_ref, xy_ref, w_ref, vg_ref, gx_ref, vx_ref,
    mix_ref, gr_ref, gk_ref, gv_ref,
    sf, sb, st, lt, packs, lowf, lowb, gr_acc, gk_acc,
):
    T, C = gr_ref.shape
    pairs = C // 128
    heads = C // HS
    count = gath_ref.shape[0]
    me = place_ref[0]
    sf[...] = jnp.zeros_like(sf)
    sb[...] = jnp.zeros_like(sb)

    def ahead(i, _):
        for h in range(heads):
            pa = gath_ref[i, h]
            sf[h] = dot3(sf[h], pa[:, :HS]) + pa[:, HS:]
        return 0

    lax.fori_loop(0, me, ahead, 0)

    def behind(i, _):
        at = count - 1 - i
        for h in range(heads):
            pa = gath_ref[at, h]
            b = gath_ref[at, heads + h // 2][:, (h % 2) * HS:(h % 2 + 1) * HS]
            sb[h] = dot3(sb[h], pa[:, :HS], NT) + b
        return 0

    lax.fori_loop(0, count - 1 - me, behind, 0)

    lane_left = iota((HS, 128), 1) < HS

    def pack(which, p, a, b):
        packs[which, 0, p] = jnp.where(lane_left, a, pltpu.roll(b, HS, 1))
        packs[which, 1, p] = jnp.where(lane_left, pltpu.roll(a, HS, 1), b)

    for p in range(pairs):
        ha, hb = 2 * p, 2 * p + 1
        along = [dot3(sf[h], xy_ref[h, :HS]) + xy_ref[h, HS:] for h in (ha, hb)]
        beta = [dot3(sb[h], w_ref[h, :HS]) + w_ref[h, HS:] for h in (ha, hb)]
        pack(0, p, *along)
        pack(1, p, *beta)
        pack(2, p, *[vg_ref[0, h * HS:(h + 1) * HS, :] for h in (ha, hb)])
        pack(3, p, *[vg_ref[1, h * HS:(h + 1) * HS, :] for h in (ha, hb)])
        st[p] = jnp.concatenate([sf[ha], sf[hb]], axis=1)
        lt[p] = jnp.concatenate([sb[ha], sb[hb]], axis=1)

    offset = jnp.where(lane_left, 0, HS)
    head_mask = (iota((8, C), 0) == iota((8, C), 1) // HS).astype(F32)
    own = iota((32, 256), 0) // 8 == iota((32, 256), 1) // HS

    def contract(base, low, by_key, left_ref, out_v, out_k):
        keys = rows_ref[by_key, pl.ds(base, 8), :]
        sums = []
        for part in range(2):
            rows32 = pl.ds(pl.multiple_of(base * 8 + part * 32, 32), 32)
            expanded = jnp.concatenate(
                [keys[j:j + 1, :] * head_mask for j in range(part * 4, part * 4 + 4)], axis=0
            ).astype(BF16)
            full = low[part * 256:(part + 1) * 256, :]
            ov = lax.dot_general(expanded, full, NT, preferred_element_type=F32)
            ov = jnp.where(own, ov, 0.0)
            ov = ov[:, :128] + ov[:, 128:]
            ov = ov + pltpu.roll(ov, HS, 1)
            out_v[rows32, :] = ov[:, :HS].astype(BF16)
            lhs = jnp.where(own, left_ref[rows32, :].astype(F32), 0.0).astype(BF16)
            ok = lax.dot_general(lhs, full, NN, preferred_element_type=F32)
            sums += [
                jnp.sum(ok[j * 8:(j + 1) * 8, :] * head_mask, axis=0, keepdims=True) for j in range(4)
            ]
        out_k[pl.ds(base, 8), :] = jnp.concatenate(sums, axis=0)

    def step(group, _):
        base = pl.multiple_of(group * 8, 8)
        base_b = pl.multiple_of(T - 8 - base, 8)
        half = base // HS
        half_b = base_b // HS
        at = offset + (base - half * HS)
        at_b = offset + (base_b - half_b * HS)
        spread = lambda a, i: jnp.take_along_axis(a, i, axis=1)
        for p in range(pairs):
            cols = slice(p * 128, (p + 1) * 128)
            rows = [rows_ref[n, pl.ds(base, 8), cols] for n in (0, 2, 4)]
            along, vals = packs[0, half, p], packs[2, half, p]
            s = st[p]
            for j in range(8):
                d, e, k = [a[j:j + 1, :] for a in rows]
                s = s * d - spread(along, at + j) * e + spread(vals, at + j) * k
                lowf[j * HS:(j + 1) * HS, cols] = s.astype(BF16)
            st[p] = s
            rows = [rows_ref[n, pl.ds(base_b, 8), cols] for n in (0, 1, 3)]
            beta, grads = packs[1, half_b, p], packs[3, half_b, p]
            c = lt[p]
            for j in reversed(range(8)):
                d, u, r = [a[j:j + 1, :] for a in rows]
                adj = c + spread(grads, at_b + j) * r
                lowb[j * HS:(j + 1) * HS, cols] = adj.astype(BF16)
                c = adj * d - spread(beta, at_b + j) * u
            lt[p] = c
        contract(base, lowf, 3, gx_ref, mix_ref, gr_acc)
        contract(base_b, lowb, 4, vx_ref, gv_ref, gk_acc)
        return 0

    lax.fori_loop(0, T // 8, step, 0)
    gr_ref[...] = gr_acc[...].astype(BF16)
    gk_ref[...] = gk_acc[...].astype(BF16)


def local(receptance, token_key, token_value, kappa_raw, removal, decay_rate, shard_length, grad_output):
    T, C = receptance.shape
    heads = C // HS
    vmem = pl.BlockSpec(memory_space=pltpu.VMEM)
    smem = pl.BlockSpec(memory_space=pltpu.SMEM)
    sds = jax.ShapeDtypeStruct
    rows, maps, xy, w, vg = pl.pallas_call(
        local_kernel,
        out_shape=(
            sds((5, T, C), F32),
            sds((heads + heads // 2, HS, 2 * HS), F32),
            sds((heads, 2 * HS, T), F32),
            sds((heads, 2 * HS, T), F32),
            sds((2, C, T), F32),
        ),
        in_specs=[smem] + [vmem] * 7,
        out_specs=(vmem,) * 5,
        compiler_params=pltpu.CompilerParams(vmem_limit_bytes=48 * 1024 * 1024),
    )(shard_length, receptance, token_key, token_value, kappa_raw, removal, decay_rate, grad_output)
    gathered = lax.all_gather(maps, "ctx")
    place = lax.axis_index("ctx").astype(jnp.int32).reshape(1)
    live = lax.broadcasted_iota(jnp.int32, (T, 1), 0) < shard_length[0]

    def spread(a):
        a = jnp.where(live, a, jnp.zeros_like(a)).reshape(T * heads, HS)
        return jnp.tile(a, (1, 4))

    mix, gr, gk, gv = pl.pallas_call(
        exact_kernel,
        out_shape=(
            sds((T * heads, HS), BF16),
            sds((T, C), BF16),
            sds((T, C), BF16),
            sds((T * heads, HS), BF16),
        ),
        in_specs=[smem] + [vmem] * 7,
        out_specs=(vmem,) * 4,
        scratch_shapes=[
            pltpu.VMEM((heads, HS, HS), F32),
            pltpu.VMEM((heads, HS, HS), F32),
            pltpu.VMEM((heads // 2, HS, 2 * HS), F32),
            pltpu.VMEM((heads // 2, HS, 2 * HS), F32),
            pltpu.VMEM((4, 2, heads // 2, HS, 2 * HS), F32),
            pltpu.VMEM((8 * HS, C), BF16),
            pltpu.VMEM((8 * HS, C), BF16),
            pltpu.VMEM((T, C), F32),
            pltpu.VMEM((T, C), F32),
        ],
        compiler_params=pltpu.CompilerParams(vmem_limit_bytes=56 * 1024 * 1024),
    )(place, gathered, rows, xy, w, vg, spread(grad_output), spread(token_value))
    return mix.reshape(T, C), gr, gk, gv.reshape(T, C)


def solution(mesh):
    both = P(("dp", "ctx"), None)
    return jax.shard_map(
        local,
        mesh=mesh,
        in_specs=(both,) * 6 + (P(("dp", "ctx")), both),
        out_specs=(both,) * 4,
        check_vma=False,
    )
```

```python
import functools

import jax
import jax.numpy as jnp
from jax import lax
from jax.experimental import pallas as pl
from jax.experimental.pallas import tpu as pltpu
from jax.sharding import PartitionSpec as P

H = 8
HS = 64
F32 = jnp.float32
BF16 = jnp.bfloat16
NN = (((1,), (0,)), ((), ()))
NT = (((1,), (1,)), ((), ()))


def halves(a):
    high = a.astype(BF16)
    return high, (a - high.astype(F32)).astype(BF16)


def dot3(a, b, dims=NN):
    ah, al = a if isinstance(a, tuple) else halves(a)
    bh, bl = b if isinstance(b, tuple) else halves(b)
    one = functools.partial(lax.dot_general, dimension_numbers=dims, preferred_element_type=F32)
    return one(ah, bh) + (one(ah, bl) + one(al, bh))


def iota(shape, dim):
    return lax.broadcasted_iota(jnp.int32, shape, dim)


def local_kernel(
    len_ref, *refs,
):
    sources, (rows_ref, maps_ref, xy_ref, w_ref, vg_ref) = refs[:7], refs[7:12]
    staged, sems = refs[12:19], refs[19]
    copies = [
        pltpu.make_async_copy(src, dst, sems.at[i]) for i, (src, dst) in enumerate(zip(sources, staged))
    ]
    for copy in copies:
        copy.start()
    for copy in copies:
        copy.wait()
    r_ref, k_ref, v_ref, kap_ref, rem_ref, rate_ref, g_ref = staged
    T, C = r_ref.shape
    live = (iota((T, 1), 0) < len_ref[0]).astype(F32)
    left = iota((T, 2 * HS), 1) < HS
    units = []
    for p in range(C // (2 * HS)):
        kap = kap_ref[:, p * 128:(p + 1) * 128].astype(F32)
        sq = kap * kap
        sa = jnp.sum(jnp.where(left, sq, 0.0), axis=1, keepdims=True)
        sb = jnp.sum(jnp.where(left, 0.0, sq), axis=1, keepdims=True)
        units.append(kap / jnp.sqrt(jnp.where(left, sa, sb) + 1e-05))
    kap = jnp.concatenate(units, axis=1)
    rate = rate_ref[...] * live
    e = rem_ref[...].astype(F32) * live * kap
    r = r_ref[...].astype(F32) * live
    k = k_ref[...].astype(F32) * live
    v = v_ref[...].astype(F32) * live
    g = g_ref[...].astype(F32) * live
    rows_ref[0] = jnp.exp(-rate)
    rows_ref[1] = kap
    rows_ref[2] = e
    rows_ref[3] = r
    rows_ref[4] = k
    rows_ref[5] = v
    rows_ref[6] = g
    tril = (iota((T, T), 0) >= iota((T, T), 1)).astype(F32)
    cs = lax.dot_general(tril, rate, NN, precision=lax.Precision.HIGHEST, preferred_element_type=F32)
    mid = cs[T // 2 - 1:T // 2, :]
    end = cs[T - 1:T, :]
    grow = jnp.exp(cs - mid)
    kap_c = kap * jnp.exp(mid - cs + rate)
    r_c = r * jnp.exp(mid - cs)
    e_ct = (e * grow).T
    k_ct = (k * grow).T
    kap_0t = (kap * jnp.exp(rate - cs)).T
    r_0t = (r * jnp.exp(-cs)).T
    to_end = jnp.exp(cs - end)
    e_end = e * to_end
    k_end = k * to_end
    e_endt = e_end.T
    vt = v.T
    gt = g.T
    vg_ref[0] = vt
    vg_ref[1] = gt
    whole = jnp.exp(-end)
    strict = iota((T, T), 0) > iota((T, T), 1)
    lower = iota((T, T), 0) >= iota((T, T), 1)
    eye = (iota((T, T), 0) == iota((T, T), 1)).astype(F32)
    eye_h = (iota((HS, HS), 0) == iota((HS, HS), 1)).astype(F32)
    heads = range(C // HS)
    row = lambda a, h: a[:, h * HS:(h + 1) * HS]
    col = lambda a, h: a[h * HS:(h + 1) * HS, :]
    low, mixes, seen = [], [], []
    for h in heads:
        both = dot3(
            jnp.concatenate([row(kap_c, h), row(r_c, h)], axis=0),
            jnp.concatenate([col(e_ct, h), col(k_ct, h)], axis=1),
        )
        low.append(jnp.where(strict, both[:T, :T], 0.0))
        mixes.append(jnp.where(strict, both[:T, T:], 0.0))
        seen.append(jnp.where(lower, both[T:, :T], 0.0))
    inverse = [eye - m for m in low]
    power = low
    size = 2
    while size < T:
        split = [halves(m) for m in power]
        power = [dot3(s, s) for s in split]
        inverse = [i + dot3(i, m) for i, m in zip(inverse, power)]
        size *= 2
    maps = []
    for h in heads:
        inv = halves(inverse[h])
        q = halves(seen[h])
        nvt = dot3(col(vt, h), mixes[h], NT)
        xy = dot3(jnp.concatenate([col(kap_0t, h), nvt], axis=0), inv, NT)
        xy_ref[h] = xy
        pa = dot3(xy, row(e_end, h))
        a = dot3(col(vt, h), row(k_end, h)) - pa[HS:]
        prod = eye_h * row(whole, h) - pa[:HS]
        zt = col(r_0t, h) - dot3(xy[:HS], q, NT)
        maps.append((a, prod, dot3(col(gt, h), zt, NT)))
        gq = dot3(col(gt, h), q)
        w_ref[h] = dot3(jnp.concatenate([col(e_endt, h), gq], axis=0), inv)
    for p in range(len(maps) // 2):
        for i in range(3):
            maps_ref[p, i] = jnp.concatenate([maps[2 * p][i], maps[2 * p + 1][i]], axis=1)


def carry_kernel(
    count, maps_ref, out_ref, member, group, incoming, states, ready,
    s1, r1, s2, r2, s3, r3,
):
    size = maps_ref.shape[0]
    groups = count // size
    me = lax.axis_index("ctx")
    q = me % size
    z = me // size
    peers = [z * size + (q + d) % size for d in range(1, size)]
    others = [((z + d) % groups) * size + q for d in range(1, groups)]
    barrier = pltpu.get_barrier_semaphore()
    for device in peers + others:
        pl.semaphore_signal(barrier, inc=1, device_id={"ctx": device}, device_id_type=pl.DeviceIdType.MESH)
    pl.semaphore_wait(barrier, len(peers) + len(others))

    def send(src, dst, send_sem, recv_sem, device):
        copy = pltpu.make_async_remote_copy(
            src_ref=src, dst_ref=dst, send_sem=send_sem, recv_sem=recv_sem,
            device_id={"ctx": device}, device_id_type=pl.DeviceIdType.MESH,
        )
        copy.start()
        return copy

    first = [
        send(maps_ref.at[(q + d) % size], member.at[q], s1.at[d - 1], r1.at[d - 1], peers[d - 1])
        for d in range(1, size)
    ]
    member[q] = maps_ref[q]
    for copy in first:
        copy.wait_recv()
    left = iota((HS, 2 * HS), 1) < HS

    def spread(m):
        return halves(jnp.concatenate([jnp.where(left, m, 0.0), jnp.where(left, 0.0, m)], axis=0))

    blocks = [spread(member[m, 1]) for m in range(size)]
    ahead = jnp.concatenate([member[0, 0], member[0, 1]], axis=0)
    back = member[size - 1, 2]
    for m in range(1, size):
        ahead = dot3(ahead, blocks[m])
        ahead = jnp.concatenate([ahead[:HS] + member[m, 0], ahead[HS:]], axis=0)
        n = size - 1 - m
        back = dot3(back, blocks[n], NT) + member[n, 2]
    group[0] = ahead[:HS]
    group[1] = ahead[HS:]
    group[2] = back
    second = []
    for d in range(1, groups):
        part = pl.ds((z + d) // groups, 2)
        second.append(
            send(group.at[part], incoming.at[z, part], s2.at[d - 1], r2.at[d - 1], others[d - 1])
        )
    for copy in second:
        copy.wait_recv()

    ready[...] = jnp.zeros_like(ready)

    def forward(i, _):
        ready[0] = dot3(ready[0], spread(incoming[i, 1])) + incoming[i, 0]
        return 0

    lax.fori_loop(0, z, forward, 0)

    def backward(i, _):
        at = groups - 1 - i
        ready[1] = dot3(ready[1], spread(incoming[at, 1]), NT) + incoming[at, 2]
        return 0

    lax.fori_loop(0, groups - 1 - z, backward, 0)
    state, adjoint = ready[0], ready[1]
    for m in range(size):
        n = size - 1 - m
        states[m, 0] = state
        states[n, 1] = adjoint
        if m < size - 1:
            state = dot3(state, blocks[m]) + member[m, 0]
            adjoint = dot3(adjoint, blocks[n], NT) + member[n, 2]
    third = [
        send(states.at[(q + d) % size], out_ref.at[q], s3.at[d - 1], r3.at[d - 1], peers[d - 1])
        for d in range(1, size)
    ]
    out_ref[q] = states[q]
    for copy in third:
        copy.wait_recv()
    for copy in first + second + third:
        copy.wait_send()


def exact_kernel(
    carry_ref, rows_ref, xy_ref, w_ref, vg_ref,
    mix_ref, gr_ref, gk_ref, gv_ref,
    st, lt, packs, lowf, lowb, mix_acc, gr_acc, gk_acc, gv_acc,
):
    T, C = gr_ref.shape
    pairs = C // 128
    lane_left = iota((HS, 128), 1) < HS

    def pack(which, p, a, b):
        packs[which, 0, p] = jnp.where(lane_left, a, pltpu.roll(b, HS, 1))
        packs[which, 1, p] = jnp.where(lane_left, pltpu.roll(a, HS, 1), b)

    for p in range(pairs):
        ha, hb = 2 * p, 2 * p + 1
        state, adjoint = carry_ref[p, 0], carry_ref[p, 1]
        cut = lambda a: (a[:, :HS], a[:, HS:])
        along = [dot3(s, xy_ref[h, :HS]) + xy_ref[h, HS:] for s, h in zip(cut(state), (ha, hb))]
        beta = [dot3(s, w_ref[h, :HS]) + w_ref[h, HS:] for s, h in zip(cut(adjoint), (ha, hb))]
        pack(0, p, *along)
        pack(1, p, *beta)
        pack(2, p, *[vg_ref[0, h * HS:(h + 1) * HS, :] for h in (ha, hb)])
        pack(3, p, *[vg_ref[1, h * HS:(h + 1) * HS, :] for h in (ha, hb)])
        st[p] = state
        lt[p] = adjoint

    offset = jnp.where(lane_left, 0, HS)
    head_mask = (iota((8, C), 0) == iota((8, C), 1) // HS).astype(F32)
    own = iota((32, 256), 0) // 8 == iota((32, 256), 1) // HS

    def contract(base, low, by_key, by_value, out_v, out_k):
        keys = rows_ref[by_key, pl.ds(base, 8), :]
        values = rows_ref[by_value, pl.ds(base, 8), :]
        sums_k, sums_v = [], []
        for part in range(2):
            spread_k, spread_v = [], []
            for j in range(part * 4, part * 4 + 4):
                spread_k.append(keys[j:j + 1, :] * head_mask)
                v8 = values[j:j + 1, :] * head_mask
                v8 = (v8[:, :128] + v8[:, 128:256]) + (v8[:, 256:384] + v8[:, 384:])
                v8 = v8 + pltpu.roll(v8, HS, 1)
                spread_v.append(jnp.concatenate([v8, v8], axis=1))
            full = low[part * 256:(part + 1) * 256, :]
            ov = lax.dot_general(
                jnp.concatenate(spread_k, axis=0).astype(BF16), full, NT, preferred_element_type=F32
            )
            ov = jnp.where(own, ov, 0.0)
            ov = ov[:, :128] + ov[:, 128:]
            ov = ov + pltpu.roll(ov, HS, 1)
            ov = jnp.concatenate([ov] * pairs, axis=1)
            lhs = jnp.where(own, jnp.concatenate(spread_v, axis=0), 0.0).astype(BF16)
            ok = lax.dot_general(lhs, full, NN, preferred_element_type=F32)
            for sums, o in ((sums_k, ok), (sums_v, ov)):
                sums += [
                    jnp.sum(o[j * 8:(j + 1) * 8, :] * head_mask, axis=0, keepdims=True)
                    for j in range(4)
                ]
        out_k[pl.ds(base, 8), :] = jnp.concatenate(sums_k, axis=0)
        out_v[pl.ds(base, 8), :] = jnp.concatenate(sums_v, axis=0)

    def step(group, _):
        base = pl.multiple_of(group * 8, 8)
        base_b = pl.multiple_of(T - 8 - base, 8)
        half = base // HS
        half_b = base_b // HS
        at = offset + (base - half * HS)
        at_b = offset + (base_b - half_b * HS)
        spread = lambda a, i: jnp.take_along_axis(a, i, axis=1)
        for p in range(pairs):
            cols = slice(p * 128, (p + 1) * 128)
            rows = [rows_ref[n, pl.ds(base, 8), cols] for n in (0, 2, 4)]
            along, vals = packs[0, half, p], packs[2, half, p]
            s = st[p]
            for j in range(8):
                d, e, k = [a[j:j + 1, :] for a in rows]
                s = s * d - spread(along, at + j) * e + spread(vals, at + j) * k
                lowf[j * HS:(j + 1) * HS, cols] = s.astype(BF16)
            st[p] = s
            rows = [rows_ref[n, pl.ds(base_b, 8), cols] for n in (0, 1, 3)]
            beta, grads = packs[1, half_b, p], packs[3, half_b, p]
            c = lt[p]
            for j in reversed(range(8)):
                d, u, r = [a[j:j + 1, :] for a in rows]
                adj = c + spread(grads, at_b + j) * r
                lowb[j * HS:(j + 1) * HS, cols] = adj.astype(BF16)
                c = adj * d - spread(beta, at_b + j) * u
            lt[p] = c
        contract(base, lowf, 3, 6, mix_acc, gr_acc)
        contract(base_b, lowb, 4, 5, gv_acc, gk_acc)
        return 0

    lax.fori_loop(0, T // 8, step, 0)
    gr_ref[...] = gr_acc[...].astype(BF16)
    gk_ref[...] = gk_acc[...].astype(BF16)
    mix_ref[...] = mix_acc[...].astype(BF16)
    gv_ref[...] = gv_acc[...].astype(BF16)


def local(receptance, token_key, token_value, kappa_raw, removal, decay_rate, shard_length, grad_output):
    T, C = receptance.shape
    heads = C // HS
    vmem = pl.BlockSpec(memory_space=pltpu.VMEM)
    smem = pl.BlockSpec(memory_space=pltpu.SMEM)
    sds = jax.ShapeDtypeStruct
    pairs = heads // 2
    arrays = (receptance, token_key, token_value, kappa_raw, removal, decay_rate, grad_output)
    rows, maps, xy, w, vg = pl.pallas_call(
        local_kernel,
        out_shape=(
            sds((7, T, C), F32),
            sds((pairs, 3, HS, 2 * HS), F32),
            sds((heads, 2 * HS, T), F32),
            sds((heads, 2 * HS, T), F32),
            sds((2, C, T), F32),
        ),
        in_specs=[smem] + [pl.BlockSpec(memory_space=pltpu.MemorySpace.HBM)] * 7,
        out_specs=(vmem,) * 5,
        scratch_shapes=[pltpu.VMEM((T, C), a.dtype) for a in arrays] + [pltpu.SemaphoreType.DMA((7,))],
        compiler_params=pltpu.CompilerParams(vmem_limit_bytes=32 * 1024 * 1024),
    )(shard_length, *arrays)
    count = lax.axis_size("ctx")
    groups = count // pairs
    dma = pltpu.SemaphoreType.DMA
    carry = pl.pallas_call(
        functools.partial(carry_kernel, count),
        out_shape=sds((pairs, 2, HS, 2 * HS), F32),
        in_specs=[vmem],
        out_specs=vmem,
        scratch_shapes=[
            pltpu.VMEM((pairs, 3, HS, 2 * HS), F32),
            pltpu.VMEM((3, HS, 2 * HS), F32),
            pltpu.VMEM((groups, 3, HS, 2 * HS), F32),
            pltpu.VMEM((pairs, 2, HS, 2 * HS), F32),
            pltpu.VMEM((2, HS, 2 * HS), F32),
            dma((pairs - 1,)), dma((pairs - 1,)),
            dma((groups - 1,)), dma((groups - 1,)),
            dma((pairs - 1,)), dma((pairs - 1,)),
        ],
        compiler_params=pltpu.CompilerParams(
            collective_id=0, has_side_effects=True, vmem_limit_bytes=32 * 1024 * 1024
        ),
    )(maps)
    return pl.pallas_call(
        exact_kernel,
        out_shape=(sds((T, C), BF16),) * 4,
        in_specs=[vmem] * 5,
        out_specs=(vmem,) * 4,
        scratch_shapes=[
            pltpu.VMEM((pairs, HS, 2 * HS), F32),
            pltpu.VMEM((pairs, HS, 2 * HS), F32),
            pltpu.VMEM((4, 2, pairs, HS, 2 * HS), F32),
            pltpu.VMEM((8 * HS, C), BF16),
            pltpu.VMEM((8 * HS, C), BF16),
        ] + [pltpu.VMEM((T, C), F32)] * 4,
        compiler_params=pltpu.CompilerParams(vmem_limit_bytes=32 * 1024 * 1024),
    )(carry, rows, xy, w, vg)


def solution(mesh):
    both = P(("dp", "ctx"), None)
    return jax.shard_map(
        local,
        mesh=mesh,
        in_specs=(both,) * 6 + (P(("dp", "ctx")), both),
        out_specs=(both,) * 4,
        check_vma=False,
    )
```

```python
import functools

import jax
import jax.numpy as jnp
from jax import lax
from jax.experimental import pallas as pl
from jax.experimental.pallas import tpu as pltpu
from jax.sharding import PartitionSpec as P

H = 8
HS = 64
F32 = jnp.float32
BF16 = jnp.bfloat16
NN = (((1,), (0,)), ((), ()))
NT = (((1,), (1,)), ((), ()))


def halves(a):
    high = a.astype(BF16)
    return high, (a - high.astype(F32)).astype(BF16)


def dot3(a, b, dims=NN):
    ah, al = a if isinstance(a, tuple) else halves(a)
    bh, bl = b if isinstance(b, tuple) else halves(b)
    one = functools.partial(lax.dot_general, dimension_numbers=dims, preferred_element_type=F32)
    return one(ah, bh) + (one(ah, bl) + one(al, bh))


def iota(shape, dim):
    return lax.broadcasted_iota(jnp.int32, shape, dim)


def local_kernel(len_ref, *refs):
    r_ref, k_ref, v_ref, kap_ref, rem_ref, rate_ref, g_ref = [refs[0].at[i] for i in range(7)]
    rows_ref, maps_ref, xy_ref, w_ref, vg_ref = refs[1:]
    T, C = r_ref.shape
    live = (iota((T, 1), 0) < len_ref[0]).astype(F32)
    left = iota((T, 2 * HS), 1) < HS
    units = []
    for p in range(C // (2 * HS)):
        kap = kap_ref[:, p * 128:(p + 1) * 128].astype(F32)
        sq = kap * kap
        sa = jnp.sum(jnp.where(left, sq, 0.0), axis=1, keepdims=True)
        sb = jnp.sum(jnp.where(left, 0.0, sq), axis=1, keepdims=True)
        units.append(kap / jnp.sqrt(jnp.where(left, sa, sb) + 1e-05))
    kap = jnp.concatenate(units, axis=1)
    rate = rate_ref[...] * live
    e = rem_ref[...].astype(F32) * live * kap
    r = r_ref[...].astype(F32) * live
    k = k_ref[...].astype(F32) * live
    v = v_ref[...].astype(F32) * live
    g = g_ref[...].astype(F32) * live
    rows_ref[0] = jnp.exp(-rate)
    rows_ref[1] = kap
    rows_ref[2] = e
    rows_ref[3] = r
    rows_ref[4] = k
    rows_ref[5] = v
    rows_ref[6] = g
    last = iota((T, 1), 0) == T - 1
    rows_ref[7] = pltpu.roll(kap, T - 1, 0)
    rows_ref[8] = jnp.where(last, 1.0, pltpu.roll(jnp.exp(-rate), T - 1, 0))
    tril = (iota((T, T), 0) >= iota((T, T), 1)).astype(F32)
    cs = lax.dot_general(tril, rate, NN, precision=lax.Precision.HIGHEST, preferred_element_type=F32)
    mid = cs[T // 2 - 1:T // 2, :]
    end = cs[T - 1:T, :]
    grow = jnp.exp(cs - mid)
    kap_c = kap * jnp.exp(mid - cs + rate)
    r_c = r * jnp.exp(mid - cs)
    e_ct = (e * grow).T
    k_ct = (k * grow).T
    kap_0t = (kap * jnp.exp(rate - cs)).T
    r_0t = (r * jnp.exp(-cs)).T
    to_end = jnp.exp(cs - end)
    e_end = e * to_end
    k_end = k * to_end
    e_endt = e_end.T
    vt = v.T
    gt = g.T
    vg_ref[0] = vt
    vg_ref[1] = gt
    whole = jnp.exp(-end)
    strict = iota((T, T), 0) > iota((T, T), 1)
    lower = iota((T, T), 0) >= iota((T, T), 1)
    eye = (iota((T, T), 0) == iota((T, T), 1)).astype(F32)
    eye_h = (iota((HS, HS), 0) == iota((HS, HS), 1)).astype(F32)
    heads = range(C // HS)
    row = lambda a, h: a[:, h * HS:(h + 1) * HS]
    col = lambda a, h: a[h * HS:(h + 1) * HS, :]
    low, mixes, seen = [], [], []
    for h in heads:
        both = dot3(
            jnp.concatenate([row(kap_c, h), row(r_c, h)], axis=0),
            jnp.concatenate([col(e_ct, h), col(k_ct, h)], axis=1),
        )
        low.append(jnp.where(strict, both[:T, :T], 0.0))
        mixes.append(jnp.where(strict, both[:T, T:], 0.0))
        seen.append(jnp.where(lower, both[T:, :T], 0.0))
    inverse = [eye - m for m in low]
    power = low
    size = 2
    while size < T:
        split = [halves(m) for m in power]
        power = [dot3(s, s) for s in split]
        inverse = [i + dot3(i, m) for i, m in zip(inverse, power)]
        size *= 2
    maps = []
    for h in heads:
        inv = halves(inverse[h])
        q = halves(seen[h])
        nvt = dot3(col(vt, h), mixes[h], NT)
        xy = dot3(jnp.concatenate([col(kap_0t, h), nvt], axis=0), inv, NT)
        xy_ref[h] = xy
        pa = dot3(xy, row(e_end, h))
        a = dot3(col(vt, h), row(k_end, h)) - pa[HS:]
        prod = eye_h * row(whole, h) - pa[:HS]
        zt = col(r_0t, h) - dot3(xy[:HS], q, NT)
        maps.append((a, prod, dot3(col(gt, h), zt, NT)))
        gq = dot3(col(gt, h), q)
        w_ref[h] = dot3(jnp.concatenate([col(e_endt, h), gq], axis=0), inv)
    for p in range(len(maps) // 2):
        for i in range(3):
            maps_ref[p, i] = jnp.concatenate([maps[2 * p][i], maps[2 * p + 1][i]], axis=1)


def carry_kernel(
    count, maps_ref, out_ref, member, group, incoming, states, ready,
    s1, r1, s2, r2, s3, r3,
):
    size = maps_ref.shape[0]
    groups = count // size
    me = lax.axis_index("ctx")
    q = me % size
    z = me // size
    peers = [z * size + (q + d) % size for d in range(1, size)]
    others = [((z + d) % groups) * size + q for d in range(1, groups)]
    barrier = pltpu.get_barrier_semaphore()
    for device in peers + others:
        pl.semaphore_signal(barrier, inc=1, device_id={"ctx": device}, device_id_type=pl.DeviceIdType.MESH)
    pl.semaphore_wait(barrier, len(peers) + len(others))

    def send(src, dst, send_sem, recv_sem, device):
        copy = pltpu.make_async_remote_copy(
            src_ref=src, dst_ref=dst, send_sem=send_sem, recv_sem=recv_sem,
            device_id={"ctx": device}, device_id_type=pl.DeviceIdType.MESH,
        )
        copy.start()
        return copy

    first = [
        send(maps_ref.at[(q + d) % size], member.at[q], s1.at[d - 1], r1.at[d - 1], peers[d - 1])
        for d in range(1, size)
    ]
    member[q] = maps_ref[q]
    for copy in first:
        copy.wait_recv()
    left = iota((HS, 2 * HS), 1) < HS

    def spread(m):
        return halves(jnp.concatenate([jnp.where(left, m, 0.0), jnp.where(left, 0.0, m)], axis=0))

    blocks = [spread(member[m, 1]) for m in range(size)]
    ahead = jnp.concatenate([member[0, 0], member[0, 1]], axis=0)
    back = member[size - 1, 2]
    for m in range(1, size):
        ahead = dot3(ahead, blocks[m])
        ahead = jnp.concatenate([ahead[:HS] + member[m, 0], ahead[HS:]], axis=0)
        n = size - 1 - m
        back = dot3(back, blocks[n], NT) + member[n, 2]
    group[0] = ahead[:HS]
    group[1] = ahead[HS:]
    group[2] = back
    second = []
    for d in range(1, groups):
        part = pl.ds((z + d) // groups, 2)
        second.append(
            send(group.at[part], incoming.at[z, part], s2.at[d - 1], r2.at[d - 1], others[d - 1])
        )
    for copy in second:
        copy.wait_recv()

    ready[...] = jnp.zeros_like(ready)

    def forward(i, _):
        ready[0] = dot3(ready[0], spread(incoming[i, 1])) + incoming[i, 0]
        return 0

    lax.fori_loop(0, z, forward, 0)

    def backward(i, _):
        at = groups - 1 - i
        ready[1] = dot3(ready[1], spread(incoming[at, 1]), NT) + incoming[at, 2]
        return 0

    lax.fori_loop(0, groups - 1 - z, backward, 0)
    state, adjoint = ready[0], ready[1]
    for m in range(size):
        n = size - 1 - m
        states[m, 0] = state
        states[n, 1] = adjoint
        if m < size - 1:
            state = dot3(state, blocks[m]) + member[m, 0]
            adjoint = dot3(adjoint, blocks[n], NT) + member[n, 2]
    third = [
        send(states.at[(q + d) % size], out_ref.at[q], s3.at[d - 1], r3.at[d - 1], peers[d - 1])
        for d in range(1, size)
    ]
    out_ref[q] = states[q]
    for copy in third:
        copy.wait_recv()
    for copy in first + second + third:
        copy.wait_send()


def exact_kernel(
    carry_ref, rows_ref, xy_ref, w_ref, vg_ref,
    mix_ref, gr_ref, gk_ref, gv_ref,
    st, lt, packs, lowf, lowb, mix_acc, gr_acc, gk_acc, gv_acc,
):
    T, C = gr_ref.shape
    pairs = C // 128
    after = iota((HS, T), 1) < T - 1
    src, dst = iota((2 * T, 2 * T), 0), iota((2 * T, 2 * T), 1)
    moved = (src % T) // 8 * 16 + src // T * 8 + src % 8
    order = (moved == dst).astype(BF16)

    def arrange(way, p, factor, exact):
        high, rest = halves(factor)
        terms = [
            lax.dot_general(m, order, NN, preferred_element_type=F32).astype(BF16)
            for m in (high, rest, exact.astype(BF16))
        ]
        for quarter in range(T // 32):
            cols = slice(quarter * HS, (quarter + 1) * HS)
            parts = [terms[i][:, cols] for i in (0, 1, 0, 2)]
            packs[way, quarter, p] = jnp.concatenate(parts, axis=1)

    for p in range(pairs):
        ha, hb = 2 * p, 2 * p + 1
        state, adjoint = carry_ref[p, 0], carry_ref[p, 1]
        cut = lambda a: (a[:, :HS], a[:, HS:])
        side = lambda a: jnp.concatenate(a, axis=1)
        along = [dot3(s, xy_ref[h, :HS]) + xy_ref[h, HS:] for s, h in zip(cut(state), (ha, hb))]
        beta = [dot3(s, w_ref[h, :HS]) + w_ref[h, HS:] for s, h in zip(cut(adjoint), (ha, hb))]
        beta = [jnp.where(after, pltpu.roll(m, T - 1, 1), 0.0) for m in beta]
        arrange(0, p, side(along), side([vg_ref[0, h * HS:(h + 1) * HS, :] for h in (ha, hb)]))
        arrange(1, p, side(beta), side([vg_ref[1, h * HS:(h + 1) * HS, :] for h in (ha, hb)]))
        st[p] = state
        lt[p] = adjoint

    head_mask = (iota((8, C), 0) == iota((8, C), 1) // HS).astype(F32)
    own = iota((32, 256), 0) // 8 == iota((32, 256), 1) // HS

    def contract(base, low, by_key, by_value, out_v, out_k):
        keys = rows_ref[by_key, pl.ds(base, 8), :]
        values = rows_ref[by_value, pl.ds(base, 8), :]
        sums_k, sums_v = [], []
        for part in range(2):
            spread_k, spread_v = [], []
            for j in range(part * 4, part * 4 + 4):
                spread_k.append(keys[j:j + 1, :] * head_mask)
                v8 = values[j:j + 1, :] * head_mask
                v8 = (v8[:, :128] + v8[:, 128:256]) + (v8[:, 256:384] + v8[:, 384:])
                v8 = v8 + pltpu.roll(v8, HS, 1)
                spread_v.append(jnp.concatenate([v8, v8], axis=1))
            full = low[part * 256:(part + 1) * 256, :]
            ov = lax.dot_general(
                jnp.concatenate(spread_k, axis=0).astype(BF16), full, NT, preferred_element_type=F32
            )
            ov = jnp.where(own, ov, 0.0)
            ov = ov[:, :128] + ov[:, 128:]
            ov = ov + pltpu.roll(ov, HS, 1)
            ov = jnp.concatenate([ov] * pairs, axis=1)
            lhs = jnp.where(own, jnp.concatenate(spread_v, axis=0), 0.0).astype(BF16)
            ok = lax.dot_general(lhs, full, NN, preferred_element_type=F32)
            for sums, o in ((sums_k, ok), (sums_v, ov)):
                sums += [
                    jnp.sum(o[j * 8:(j + 1) * 8, :] * head_mask, axis=0, keepdims=True)
                    for j in range(4)
                ]
        out_k[pl.ds(base, 8), :] = jnp.concatenate(sums_k, axis=0)
        out_v[pl.ds(base, 8), :] = jnp.concatenate(sums_v, axis=0)

    r16, l16 = iota((16, 128), 0), iota((16, 128), 1)
    picks = [(r16 // 8 == l16 // HS) & (r16 % 8 == j) for j in range(8)]
    none = jnp.zeros((16, 128), BF16)

    def fresh(way, quarter, octet, p, factors, exacts):
        columns = []
        for j in range(8):
            high, rest = halves(jnp.where(picks[j], -factors[j:j + 1, :], 0.0))
            exact = jnp.where(picks[j], exacts[j:j + 1, :], 0.0).astype(BF16)
            blocks = []
            for term in (high, high, rest, exact):
                blocks += [term if at == octet else none for at in range(4)]
            columns.append(jnp.concatenate(blocks, axis=0))
        weights = jnp.concatenate(columns, axis=1)
        return lax.dot_general(packs[way, quarter, p], weights, NN, preferred_element_type=F32)

    def quarters(quarter, _):
        quarter_b = T // 32 - 1 - quarter
        for octet in range(4):
            octet_b = 3 - octet
            base = pl.multiple_of(quarter * 32 + octet * 8, 8)
            base_b = pl.multiple_of(quarter_b * 32 + octet_b * 8, 8)
            for p in range(pairs):
                cols = slice(p * 128, (p + 1) * 128)
                d, e, k = [rows_ref[n, pl.ds(base, 8), cols] for n in (0, 2, 4)]
                new = fresh(0, quarter, octet, p, e, k)
                s = st[p]
                for j in range(8):
                    s = s * d[j:j + 1, :] + new[:, j * 128:(j + 1) * 128]
                    lowf[j * HS:(j + 1) * HS, cols] = s.astype(BF16)
                st[p] = s
                d, u, r = [rows_ref[n, pl.ds(base_b, 8), cols] for n in (8, 7, 3)]
                new = fresh(1, quarter_b, octet_b, p, u, r)
                c = lt[p]
                for j in reversed(range(8)):
                    c = c * d[j:j + 1, :] + new[:, j * 128:(j + 1) * 128]
                    lowb[j * HS:(j + 1) * HS, cols] = c.astype(BF16)
                lt[p] = c
            contract(base, lowf, 3, 6, mix_acc, gr_acc)
            contract(base_b, lowb, 4, 5, gv_acc, gk_acc)
        return 0

    lax.fori_loop(0, T // 32, quarters, 0)
    gr_ref[...] = gr_acc[...].astype(BF16)
    gk_ref[...] = gk_acc[...].astype(BF16)
    mix_ref[...] = mix_acc[...].astype(BF16)
    gv_ref[...] = gv_acc[...].astype(BF16)


def local(receptance, token_key, token_value, kappa_raw, removal, decay_rate, shard_length, grad_output):
    T, C = receptance.shape
    heads = C // HS
    vmem = pl.BlockSpec(memory_space=pltpu.VMEM)
    smem = pl.BlockSpec(memory_space=pltpu.SMEM)
    sds = jax.ShapeDtypeStruct
    pairs = heads // 2
    arrays = (receptance, token_key, token_value, kappa_raw, removal, decay_rate, grad_output)
    which = lax.broadcasted_iota(jnp.int32, (len(arrays), T, C), 0)
    together = jnp.zeros((len(arrays), T, C), F32)
    for i, a in enumerate(arrays):
        together = jnp.where(which == i, a.astype(F32)[None], together)
    rows, maps, xy, w, vg = pl.pallas_call(
        local_kernel,
        out_shape=(
            sds((9, T, C), F32),
            sds((pairs, 3, HS, 2 * HS), F32),
            sds((heads, 2 * HS, T), F32),
            sds((heads, 2 * HS, T), F32),
            sds((2, C, T), F32),
        ),
        in_specs=[smem, vmem],
        out_specs=(vmem,) * 5,
        compiler_params=pltpu.CompilerParams(vmem_limit_bytes=32 * 1024 * 1024),
    )(shard_length, together)
    count = lax.axis_size("ctx")
    groups = count // pairs
    dma = pltpu.SemaphoreType.DMA
    carry = pl.pallas_call(
        functools.partial(carry_kernel, count),
        out_shape=sds((pairs, 2, HS, 2 * HS), F32),
        in_specs=[vmem],
        out_specs=vmem,
        scratch_shapes=[
            pltpu.VMEM((pairs, 3, HS, 2 * HS), F32),
            pltpu.VMEM((3, HS, 2 * HS), F32),
            pltpu.VMEM((groups, 3, HS, 2 * HS), F32),
            pltpu.VMEM((pairs, 2, HS, 2 * HS), F32),
            pltpu.VMEM((2, HS, 2 * HS), F32),
            dma((pairs - 1,)), dma((pairs - 1,)),
            dma((groups - 1,)), dma((groups - 1,)),
            dma((pairs - 1,)), dma((pairs - 1,)),
        ],
        compiler_params=pltpu.CompilerParams(
            collective_id=0, has_side_effects=True, vmem_limit_bytes=32 * 1024 * 1024
        ),
    )(maps)
    return pl.pallas_call(
        exact_kernel,
        out_shape=(sds((T, C), BF16),) * 4,
        in_specs=[vmem] * 5,
        out_specs=(vmem,) * 4,
        scratch_shapes=[
            pltpu.VMEM((pairs, HS, 2 * HS), F32),
            pltpu.VMEM((pairs, HS, 2 * HS), F32),
            pltpu.VMEM((2, T // 32, pairs, HS, 4 * HS), BF16),
            pltpu.VMEM((8 * HS, C), BF16),
            pltpu.VMEM((8 * HS, C), BF16),
        ] + [pltpu.VMEM((T, C), F32)] * 4,
        compiler_params=pltpu.CompilerParams(vmem_limit_bytes=32 * 1024 * 1024),
    )(carry, rows, xy, w, vg)


def solution(mesh):
    both = P(("dp", "ctx"), None)
    return jax.shard_map(
        local,
        mesh=mesh,
        in_specs=(both,) * 6 + (P(("dp", "ctx")), both),
        out_specs=(both,) * 4,
        check_vma=False,
    )
```

```python
import functools

import jax
import jax.numpy as jnp
from jax import lax
from jax.experimental import pallas as pl
from jax.experimental.pallas import tpu as pltpu
from jax.sharding import PartitionSpec as P

H = 8
HS = 64
F32 = jnp.float32
BF16 = jnp.bfloat16
NN = (((1,), (0,)), ((), ()))
NT = (((1,), (1,)), ((), ()))


def halves(a):
    high = a.astype(BF16)
    return high, (a - high.astype(F32)).astype(BF16)


def dot3(a, b, dims=NN):
    ah, al = a if isinstance(a, tuple) else halves(a)
    bh, bl = b if isinstance(b, tuple) else halves(b)
    one = functools.partial(lax.dot_general, dimension_numbers=dims, preferred_element_type=F32)
    return one(ah, bh) + (one(ah, bl) + one(al, bh))


def iota(shape, dim):
    return lax.broadcasted_iota(jnp.int32, shape, dim)


def local_kernel(len_ref, *refs):
    r_ref, k_ref, v_ref, kap_ref, rem_ref, g_ref = [refs[0].at[i] for i in range(6)]
    rate_ref = refs[1]
    rows_ref, maps_ref, xy_ref, w_ref, vg_ref = refs[2:]
    T, C = r_ref.shape
    live = (iota((T, 1), 0) < len_ref[0]).astype(F32)
    left = iota((T, 2 * HS), 1) < HS
    units = []
    for p in range(C // (2 * HS)):
        kap = kap_ref[:, p * 128:(p + 1) * 128].astype(F32)
        sq = kap * kap
        sa = jnp.sum(jnp.where(left, sq, 0.0), axis=1, keepdims=True)
        sb = jnp.sum(jnp.where(left, 0.0, sq), axis=1, keepdims=True)
        units.append(kap / jnp.sqrt(jnp.where(left, sa, sb) + 1e-05))
    kap = jnp.concatenate(units, axis=1)
    rate = rate_ref[...] * live
    e = rem_ref[...].astype(F32) * live * kap
    r = r_ref[...].astype(F32) * live
    k = k_ref[...].astype(F32) * live
    v = v_ref[...].astype(F32) * live
    g = g_ref[...].astype(F32) * live
    rows_ref[0] = jnp.exp(-rate)
    rows_ref[1] = kap
    rows_ref[2] = e
    rows_ref[3] = r
    rows_ref[4] = k
    rows_ref[5] = v
    rows_ref[6] = g
    last = iota((T, 1), 0) == T - 1
    rows_ref[7] = pltpu.roll(kap, T - 1, 0)
    rows_ref[8] = jnp.where(last, 1.0, pltpu.roll(jnp.exp(-rate), T - 1, 0))
    tril = (iota((T, T), 0) >= iota((T, T), 1)).astype(F32)
    cs = lax.dot_general(tril, rate, NN, precision=lax.Precision.HIGHEST, preferred_element_type=F32)
    mid = cs[T // 2 - 1:T // 2, :]
    end = cs[T - 1:T, :]
    grow = jnp.exp(cs - mid)
    kap_c = kap * jnp.exp(mid - cs + rate)
    r_c = r * jnp.exp(mid - cs)
    e_ct = (e * grow).T
    k_ct = (k * grow).T
    kap_0t = (kap * jnp.exp(rate - cs)).T
    r_0t = (r * jnp.exp(-cs)).T
    to_end = jnp.exp(cs - end)
    e_end = e * to_end
    k_end = k * to_end
    e_endt = e_end.T
    vt = v.T
    gt = g.T
    vg_ref[0] = vt
    vg_ref[1] = gt
    whole = jnp.exp(-end)
    strict = iota((T, T), 0) > iota((T, T), 1)
    lower = iota((T, T), 0) >= iota((T, T), 1)
    eye = (iota((T, T), 0) == iota((T, T), 1)).astype(F32)
    eye_h = (iota((HS, HS), 0) == iota((HS, HS), 1)).astype(F32)
    heads = range(C // HS)
    row = lambda a, h: a[:, h * HS:(h + 1) * HS]
    col = lambda a, h: a[h * HS:(h + 1) * HS, :]
    low, mixes, seen = [], [], []
    for h in heads:
        both = dot3(
            jnp.concatenate([row(kap_c, h), row(r_c, h)], axis=0),
            jnp.concatenate([col(e_ct, h), col(k_ct, h)], axis=1),
        )
        low.append(jnp.where(strict, both[:T, :T], 0.0))
        mixes.append(jnp.where(strict, both[:T, T:], 0.0))
        seen.append(jnp.where(lower, both[T:, :T], 0.0))
    inverse = [eye - m for m in low]
    power = low
    size = 2
    while size < T:
        split = [halves(m) for m in power]
        power = [dot3(s, s) for s in split]
        inverse = [i + dot3(i, m) for i, m in zip(inverse, power)]
        size *= 2
    maps = []
    for h in heads:
        inv = halves(inverse[h])
        q = halves(seen[h])
        nvt = dot3(col(vt, h), mixes[h], NT)
        xy = dot3(jnp.concatenate([col(kap_0t, h), nvt], axis=0), inv, NT)
        xy_ref[h] = xy
        pa = dot3(xy, row(e_end, h))
        a = dot3(col(vt, h), row(k_end, h)) - pa[HS:]
        prod = eye_h * row(whole, h) - pa[:HS]
        zt = col(r_0t, h) - dot3(xy[:HS], q, NT)
        maps.append((a, prod, dot3(col(gt, h), zt, NT)))
        gq = dot3(col(gt, h), q)
        w_ref[h] = dot3(jnp.concatenate([col(e_endt, h), gq], axis=0), inv)
    for p in range(len(maps) // 2):
        for i in range(3):
            maps_ref[p, i] = jnp.concatenate([maps[2 * p][i], maps[2 * p + 1][i]], axis=1)


def carry_kernel(
    count, maps_ref, out_ref, member, group, incoming, states, ready,
    s1, r1, s2, r2, s3, r3,
):
    size = maps_ref.shape[0]
    groups = count // size
    me = lax.axis_index("ctx")
    q = me % size
    z = me // size
    peers = [z * size + (q + d) % size for d in range(1, size)]
    others = [((z + d) % groups) * size + q for d in range(1, groups)]
    barrier = pltpu.get_barrier_semaphore()
    for device in peers + others:
        pl.semaphore_signal(barrier, inc=1, device_id={"ctx": device}, device_id_type=pl.DeviceIdType.MESH)
    pl.semaphore_wait(barrier, len(peers) + len(others))

    def send(src, dst, send_sem, recv_sem, device):
        copy = pltpu.make_async_remote_copy(
            src_ref=src, dst_ref=dst, send_sem=send_sem, recv_sem=recv_sem,
            device_id={"ctx": device}, device_id_type=pl.DeviceIdType.MESH,
        )
        copy.start()
        return copy

    first = [
        send(maps_ref.at[(q + d) % size], member.at[q], s1.at[d - 1], r1.at[d - 1], peers[d - 1])
        for d in range(1, size)
    ]
    member[q] = maps_ref[q]
    for copy in first:
        copy.wait_recv()
    left = iota((HS, 2 * HS), 1) < HS

    def spread(m):
        return halves(jnp.concatenate([jnp.where(left, m, 0.0), jnp.where(left, 0.0, m)], axis=0))

    blocks = [spread(member[m, 1]) for m in range(size)]
    ahead = jnp.concatenate([member[0, 0], member[0, 1]], axis=0)
    back = member[size - 1, 2]
    for m in range(1, size):
        ahead = dot3(ahead, blocks[m])
        ahead = jnp.concatenate([ahead[:HS] + member[m, 0], ahead[HS:]], axis=0)
        n = size - 1 - m
        back = dot3(back, blocks[n], NT) + member[n, 2]
    group[0] = ahead[:HS]
    group[1] = ahead[HS:]
    group[2] = back
    second = []
    for d in range(1, groups):
        part = pl.ds((z + d) // groups, 2)
        second.append(
            send(group.at[part], incoming.at[z, part], s2.at[d - 1], r2.at[d - 1], others[d - 1])
        )
    for copy in second:
        copy.wait_recv()

    ready[...] = jnp.zeros_like(ready)

    def forward(i, _):
        ready[0] = dot3(ready[0], spread(incoming[i, 1])) + incoming[i, 0]
        return 0

    lax.fori_loop(0, z, forward, 0)

    def backward(i, _):
        at = groups - 1 - i
        ready[1] = dot3(ready[1], spread(incoming[at, 1]), NT) + incoming[at, 2]
        return 0

    lax.fori_loop(0, groups - 1 - z, backward, 0)
    state, adjoint = ready[0], ready[1]
    for m in range(size):
        n = size - 1 - m
        states[m, 0] = state
        states[n, 1] = adjoint
        if m < size - 1:
            state = dot3(state, blocks[m]) + member[m, 0]
            adjoint = dot3(adjoint, blocks[n], NT) + member[n, 2]
    third = [
        send(states.at[(q + d) % size], out_ref.at[q], s3.at[d - 1], r3.at[d - 1], peers[d - 1])
        for d in range(1, size)
    ]
    out_ref[q] = states[q]
    for copy in third:
        copy.wait_recv()
    for copy in first + second + third:
        copy.wait_send()


def exact_kernel(
    carry_ref, rows_ref, xy_ref, w_ref, vg_ref,
    mix_ref, gr_ref, gk_ref, gv_ref,
    st, lt, packs, lowf, lowb, mix_acc, gr_acc, gk_acc, gv_acc,
):
    T, C = gr_ref.shape
    pairs = C // 128
    after = iota((HS, T), 1) < T - 1
    src, dst = iota((2 * T, 2 * T), 0), iota((2 * T, 2 * T), 1)
    moved = (src % T) // 8 * 16 + src // T * 8 + src % 8
    order = (moved == dst).astype(BF16)

    def arrange(way, p, factor, exact):
        high, rest = halves(factor)
        terms = [
            lax.dot_general(m, order, NN, preferred_element_type=F32).astype(BF16)
            for m in (high, rest, exact.astype(BF16))
        ]
        for quarter in range(T // 32):
            cols = slice(quarter * HS, (quarter + 1) * HS)
            parts = [terms[i][:, cols] for i in (0, 1, 0, 2)]
            packs[way, quarter, p] = jnp.concatenate(parts, axis=1)

    for p in range(pairs):
        ha, hb = 2 * p, 2 * p + 1
        state, adjoint = carry_ref[p, 0], carry_ref[p, 1]
        cut = lambda a: (a[:, :HS], a[:, HS:])
        side = lambda a: jnp.concatenate(a, axis=1)
        along = [dot3(s, xy_ref[h, :HS]) + xy_ref[h, HS:] for s, h in zip(cut(state), (ha, hb))]
        beta = [dot3(s, w_ref[h, :HS]) + w_ref[h, HS:] for s, h in zip(cut(adjoint), (ha, hb))]
        beta = [jnp.where(after, pltpu.roll(m, T - 1, 1), 0.0) for m in beta]
        arrange(0, p, side(along), side([vg_ref[0, h * HS:(h + 1) * HS, :] for h in (ha, hb)]))
        arrange(1, p, side(beta), side([vg_ref[1, h * HS:(h + 1) * HS, :] for h in (ha, hb)]))
        st[p] = state
        lt[p] = adjoint

    head_mask = (iota((8, C), 0) == iota((8, C), 1) // HS).astype(F32)
    own = iota((32, 256), 0) // 8 == iota((32, 256), 1) // HS

    def contract(base, low, by_key, by_value, out_v, out_k):
        keys = rows_ref[by_key, pl.ds(base, 8), :]
        values = rows_ref[by_value, pl.ds(base, 8), :]
        sums_k, sums_v = [], []
        for part in range(2):
            spread_k, spread_v = [], []
            for j in range(part * 4, part * 4 + 4):
                spread_k.append(keys[j:j + 1, :] * head_mask)
                v8 = values[j:j + 1, :] * head_mask
                v8 = (v8[:, :128] + v8[:, 128:256]) + (v8[:, 256:384] + v8[:, 384:])
                v8 = v8 + pltpu.roll(v8, HS, 1)
                spread_v.append(jnp.concatenate([v8, v8], axis=1))
            full = low[part * 256:(part + 1) * 256, :]
            ov = lax.dot_general(
                jnp.concatenate(spread_k, axis=0).astype(BF16), full, NT, preferred_element_type=F32
            )
            ov = jnp.where(own, ov, 0.0)
            ov = ov[:, :128] + ov[:, 128:]
            ov = ov + pltpu.roll(ov, HS, 1)
            ov = jnp.concatenate([ov] * pairs, axis=1)
            lhs = jnp.where(own, jnp.concatenate(spread_v, axis=0), 0.0).astype(BF16)
            ok = lax.dot_general(lhs, full, NN, preferred_element_type=F32)
            for sums, o in ((sums_k, ok), (sums_v, ov)):
                sums += [
                    jnp.sum(o[j * 8:(j + 1) * 8, :] * head_mask, axis=0, keepdims=True)
                    for j in range(4)
                ]
        out_k[pl.ds(base, 8), :] = jnp.concatenate(sums_k, axis=0)
        out_v[pl.ds(base, 8), :] = jnp.concatenate(sums_v, axis=0)

    r16, l16 = iota((16, 128), 0), iota((16, 128), 1)
    picks = [(r16 // 8 == l16 // HS) & (r16 % 8 == j) for j in range(8)]
    none = jnp.zeros((16, 128), BF16)

    def fresh(way, quarter, octet, p, factors, exacts):
        columns = []
        for j in range(8):
            high, rest = halves(jnp.where(picks[j], -factors[j:j + 1, :], 0.0))
            exact = jnp.where(picks[j], exacts[j:j + 1, :], 0.0).astype(BF16)
            blocks = []
            for term in (high, high, rest, exact):
                blocks += [term if at == octet else none for at in range(4)]
            columns.append(jnp.concatenate(blocks, axis=0))
        weights = jnp.concatenate(columns, axis=1)
        return lax.dot_general(packs[way, quarter, p], weights, NN, preferred_element_type=F32)

    def quarters(quarter, _):
        quarter_b = T // 32 - 1 - quarter
        for octet in range(4):
            octet_b = 3 - octet
            base = pl.multiple_of(quarter * 32 + octet * 8, 8)
            base_b = pl.multiple_of(quarter_b * 32 + octet_b * 8, 8)
            for p in range(pairs):
                cols = slice(p * 128, (p + 1) * 128)
                d, e, k = [rows_ref[n, pl.ds(base, 8), cols] for n in (0, 2, 4)]
                new = fresh(0, quarter, octet, p, e, k)
                s = st[p]
                for j in range(8):
                    s = s * d[j:j + 1, :] + new[:, j * 128:(j + 1) * 128]
                    lowf[j * HS:(j + 1) * HS, cols] = s.astype(BF16)
                st[p] = s
                d, u, r = [rows_ref[n, pl.ds(base_b, 8), cols] for n in (8, 7, 3)]
                new = fresh(1, quarter_b, octet_b, p, u, r)
                c = lt[p]
                for j in reversed(range(8)):
                    c = c * d[j:j + 1, :] + new[:, j * 128:(j + 1) * 128]
                    lowb[j * HS:(j + 1) * HS, cols] = c.astype(BF16)
                lt[p] = c
            contract(base, lowf, 3, 6, mix_acc, gr_acc)
            contract(base_b, lowb, 4, 5, gv_acc, gk_acc)
        return 0

    lax.fori_loop(0, T // 32, quarters, 0)
    gr_ref[...] = gr_acc[...].astype(BF16)
    gk_ref[...] = gk_acc[...].astype(BF16)
    mix_ref[...] = mix_acc[...].astype(BF16)
    gv_ref[...] = gv_acc[...].astype(BF16)


def local(receptance, token_key, token_value, kappa_raw, removal, decay_rate, shard_length, grad_output):
    T, C = receptance.shape
    heads = C // HS
    vmem = pl.BlockSpec(memory_space=pltpu.VMEM)
    smem = pl.BlockSpec(memory_space=pltpu.SMEM)
    sds = jax.ShapeDtypeStruct
    pairs = heads // 2
    arrays = (receptance, token_key, token_value, kappa_raw, removal, grad_output)
    which = lax.broadcasted_iota(jnp.int32, (len(arrays), T, C), 0)
    together = jnp.zeros((len(arrays), T, C), BF16)
    for i, a in enumerate(arrays):
        together = jnp.where(which == i, a[None], together)
    rows, maps, xy, w, vg = pl.pallas_call(
        local_kernel,
        out_shape=(
            sds((9, T, C), F32),
            sds((pairs, 3, HS, 2 * HS), F32),
            sds((heads, 2 * HS, T), F32),
            sds((heads, 2 * HS, T), F32),
            sds((2, C, T), F32),
        ),
        in_specs=[smem, vmem, vmem],
        out_specs=(vmem,) * 5,
        compiler_params=pltpu.CompilerParams(vmem_limit_bytes=32 * 1024 * 1024),
    )(shard_length, together, decay_rate)
    count = lax.axis_size("ctx")
    groups = count // pairs
    dma = pltpu.SemaphoreType.DMA
    carry = pl.pallas_call(
        functools.partial(carry_kernel, count),
        out_shape=sds((pairs, 2, HS, 2 * HS), F32),
        in_specs=[vmem],
        out_specs=vmem,
        scratch_shapes=[
            pltpu.VMEM((pairs, 3, HS, 2 * HS), F32),
            pltpu.VMEM((3, HS, 2 * HS), F32),
            pltpu.VMEM((groups, 3, HS, 2 * HS), F32),
            pltpu.VMEM((pairs, 2, HS, 2 * HS), F32),
            pltpu.VMEM((2, HS, 2 * HS), F32),
            dma((pairs - 1,)), dma((pairs - 1,)),
            dma((groups - 1,)), dma((groups - 1,)),
            dma((pairs - 1,)), dma((pairs - 1,)),
        ],
        compiler_params=pltpu.CompilerParams(
            collective_id=0, has_side_effects=True, vmem_limit_bytes=32 * 1024 * 1024
        ),
    )(maps)
    return pl.pallas_call(
        exact_kernel,
        out_shape=(sds((T, C), BF16),) * 4,
        in_specs=[vmem] * 5,
        out_specs=(vmem,) * 4,
        scratch_shapes=[
            pltpu.VMEM((pairs, HS, 2 * HS), F32),
            pltpu.VMEM((pairs, HS, 2 * HS), F32),
            pltpu.VMEM((2, T // 32, pairs, HS, 4 * HS), BF16),
            pltpu.VMEM((8 * HS, C), BF16),
            pltpu.VMEM((8 * HS, C), BF16),
        ] + [pltpu.VMEM((T, C), F32)] * 4,
        compiler_params=pltpu.CompilerParams(vmem_limit_bytes=32 * 1024 * 1024),
    )(carry, rows, xy, w, vg)


def solution(mesh):
    both = P(("dp", "ctx"), None)
    return jax.shard_map(
        local,
        mesh=mesh,
        in_specs=(both,) * 6 + (P(("dp", "ctx")), both),
        out_specs=(both,) * 4,
        check_vma=False,
    )
```
